32 devices in a mesh: section: 2 (over x), tensor: 4 (over y, core), dp: 4 (over z).
Axes of the slice: x: 2, y: 2, z: 4, core: 2. Of those that a mesh axis runs over, the one named last changes fastest.
Arguments:
- tokens: bfloat16 [3, 512, 768], P(None, 'dp'), may hold values from -3 to 3
- block_order: int32 [3, 4], replicated, may hold values from 0 to 3, each once within a row
- ln_gain: float32 [2, 2, 768], P('section'), may hold values from 0.5 to 1.5
- ln_bias: float32 [2, 2, 768], P('section'), may hold values from -0.75 to 0.75
- qkv_weight: bfloat16 [2, 768, 3, 768], P('section', None, None, 'tensor'), may hold values from -0.12597656 to 0.12597656
- qv_bias: float32 [2, 2, 768], P('section', None, 'tensor'), may hold values from -0.75 to 0.75
- out_weight: bfloat16 [2, 768, 768], P('section', 'tensor'), may hold values from -0.3125 to 0.3125
- out_bias: float32 [2, 768], P('section'), may hold values from -0.75 to 0.75
- fc_weight: bfloat16 [2, 768, 3072], P('section', None, 'tensor'), may hold values from -0.21875 to 0.21875
- fc_bias: float32 [2, 3072], P('section', 'tensor'), may hold values from -0.75 to 0.75
- proj_weight: bfloat16 [2, 3072, 768], P('section', 'tensor'), may hold values from -0.109375 to 0.109375
- proj_bias: float32 [2, 768], P('section'), may hold values from -0.75 to 0.75
- cotangent: bfloat16 [3, 512, 768], P(None, 'dp'), may hold values from -3 to 3
Outputs:
- section_out: bfloat16 [2, 3, 512, 768], P('section', None, 'dp')
- section_grad: float32 [2, 3, 512, 768], P('section', None, 'dp')
- grad_ln_gain: float32 [2, 2, 768], P('section')
- grad_ln_bias: float32 [2, 2, 768], P('section')
- grad_qkv_weight: float32 [2, 768, 3, 768], P('section', None, None, 'tensor')
- grad_qv_bias: float32 [2, 2, 768], P('section', None, 'tensor')
- grad_out_weight: float32 [2, 768, 768], P('section', 'tensor')
- grad_out_bias: float32 [2, 768], P('section')
- grad_fc_weight: float32 [2, 768, 3072], P('section', None, 'tensor')
- grad_fc_bias: float32 [2, 3072], P('section', 'tensor')
- grad_proj_weight: float32 [2, 3072, 768], P('section', 'tensor')
- grad_proj_bias: float32 [2, 768], P('section')
The draws below stay inside these ranges and needn't reach their ends.
Inputs may be any that keep to these rules, and one draw needn't show every extreme that they name: Each row is a permutation: index j of dp holds the positions from 128 * block_order[m, j] on.
All inputs are finite; a program needn't handle non-finite values.
Results may differ from the reference program's by a relative error of at most 0.025.
The reference program's roundings to bfloat16 on the way count: a program that leaves them out, or rounds other values in their place, can miss the bound.
Values may be sent and summed in bfloat16 or wider, within the bound.
A program may use at most 128 MiB of HBM per device.

```python
import math
import jax
import jax.numpy as jnp
from jax import lax

D = 768
HEADS = 12
HEAD = 64
FF = 3072
MB_DEV = 128
MICRO = 3
BLOCKS = 4
LENGTH = 512


def steps_of(own_key, extent, shards, smallest, top_value):
    factor_of = 1.0
    for dim, parts in shards:
        draws = jax.random.uniform(jax.random.fold_in(jax.random.fold_in(own_key, 6), dim), (parts,), jnp.float32, smallest / len(shards), top_value / len(shards))
        factor_of = factor_of * jnp.repeat(jnp.exp(draws), extent[dim] // parts).reshape((-1,) + (1,) * (len(extent) - 1 - dim))
    return factor_of


def normal_values(stream_key, extent, width, limit, pieces=(), kind=jnp.bfloat16):
    gain = steps_of(stream_key, extent, pieces, -0.22, 0.18) if pieces else 1.0
    array = jax.random.normal(stream_key, extent, jnp.float32) * width * gain
    return jnp.minimum(jnp.maximum(array, -limit), limit).astype(kind)


def setup_inputs(seed: int = 0) -> dict:
    seeds = jax.random.split(jax.random.key(seed), 14)
    return {
        "tokens": normal_values(seeds[0], (MICRO, LENGTH, D), 1.0, 3.0, ((1, 4),)),
        "block_order": jax.vmap(lambda own: jax.random.permutation(own, BLOCKS))(jax.random.split(seeds[1], MICRO)).reshape((MICRO, BLOCKS)).astype(jnp.int32),
        "ln_gain": jnp.clip(1.0 + 0.1 * jax.random.normal(seeds[2], (2, 2, D), jnp.float32), 0.5, 1.5),
        "ln_bias": normal_values(seeds[3], (2, 2, D), 0.3, 0.75, ((0, 2),), jnp.float32),
        "qkv_weight": normal_values(seeds[4], (2, D, 3, D), (1.4 / D ** 0.5), 0.12597656, ((0, 2), (3, 4))),
        "qv_bias": normal_values(seeds[5], (2, 2, D), 0.3, 0.75, ((0, 2), (2, 4)), jnp.float32),
        "out_weight": normal_values(seeds[6], (2, D, D), (D // 2) ** -0.5, 0.3125, ((0, 2), (1, 4))),
        "out_bias": normal_values(seeds[7], (2, D), 0.3, 0.75, ((0, 2),), jnp.float32),
        "fc_weight": normal_values(seeds[8], (2, D, FF), D ** -0.5, 0.21875, ((0, 2), (2, 4))),
        "fc_bias": normal_values(seeds[9], (2, FF), 0.3, 0.75, ((0, 2), (1, 4)), jnp.float32),
        "proj_weight": normal_values(seeds[10], (2, FF, D), FF ** -0.5, 0.109375, ((0, 2), (1, 4))),
        "proj_bias": normal_values(seeds[11], (2, D), 0.3, 0.75, ((0, 2),), jnp.float32),
        "cotangent": normal_values(seeds[12], (MICRO, LENGTH, D), 1.0, 3.0, ((1, 4),)),
    }


@jax.custom_vjp
def low(v):
    return lax.optimization_barrier(v.astype(jnp.bfloat16)).astype(jnp.float32)

@jax.custom_vjp
def low_back(v):
    return v

def low_keep(v):
    return (low(v), None)

def low_pass(kept, grad):
    return (grad,)

def back_keep(v):
    return (v, None)

def back_low(kept, grad):
    return (low(grad),)
low.defvjp(low_keep, low_pass)
low_back.defvjp(back_keep, back_low)
EPSILON = 1e-05
MASKED = -1e+30
GELU_RATE = 0.7978845608028654
GELU_CUBE = 0.044715

def layer_norm(values, gains, biases):
    average = lax.optimization_barrier(jnp.mean(values, axis=-1, keepdims=True))
    centered = values - average
    spread = lax.optimization_barrier(jnp.mean(centered * centered, axis=-1, keepdims=True))
    return centered * lax.rsqrt(spread + EPSILON) * gains + biases

def gelu_tanh(values):
    return 0.5 * values * (1.0 + jnp.tanh(GELU_RATE * (values + GELU_CUBE * values * values * values)))

def matmul(left, right):
    return jnp.dot(left, right, precision=lax.Precision.HIGHEST, preferred_element_type=jnp.float32)

def layer(inputs, positions, gains, biases, qkv_weight, qv_bias, out_weight, out_bias, fc_weight, fc_bias, proj_weight, proj_bias):
    normed = low(layer_norm(inputs, gains[0], biases[0]))
    projected = matmul(normed, qkv_weight.reshape(D, 3 * D))
    query = low(low_back(projected[:, :D] + qv_bias[0]))
    keys = low(low_back(projected[:, D:2 * D]))
    values = low(low_back(projected[:, 2 * D:] + qv_bias[1]))
    key_heads = keys.reshape(LENGTH, HEADS, HEAD)
    value_heads = values.reshape(LENGTH, HEADS, HEAD)

    def attend_block(operands):
        query_block, position_block = operands
        scores = jnp.einsum('qhe,khe->hqk', query_block, key_heads, precision=lax.Precision.HIGHEST) * (1.0 / math.sqrt(HEAD))
        scores = low_back(scores)
        allowed = (position_block[:, None] >= positions[None, :])[None, :, :]
        softmax = low(jax.nn.softmax(jnp.where(allowed, scores, MASKED), axis=-1))
        return jnp.einsum('hqk,khe->qhe', softmax, value_heads, precision=lax.Precision.HIGHEST)
    query_blocks = query.reshape(LENGTH // MB_DEV, MB_DEV, HEADS, HEAD)
    position_blocks = positions.reshape(LENGTH // MB_DEV, MB_DEV)
    attended = lax.map(jax.checkpoint(attend_block), (query_blocks, position_blocks)).reshape(LENGTH, D)
    attended = low(low_back(attended))
    middle = inputs + low_back(matmul(attended, out_weight)) + out_bias
    normed_mid = low(layer_norm(middle, gains[1], biases[1]))
    hidden_pre = low_back(matmul(normed_mid, fc_weight) + fc_bias)
    active = low(gelu_tanh(hidden_pre))
    return middle + low_back(matmul(active, proj_weight)) + proj_bias

def reference(tokens, block_order, ln_gain, ln_bias, qkv_weight, qv_bias, out_weight, out_bias, fc_weight, fc_bias, proj_weight, proj_bias, cotangent):
    row_index = jnp.arange(LENGTH, dtype=jnp.int32)
    positions = block_order[:, row_index // MB_DEV] * MB_DEV + row_index % MB_DEV
    weights = (ln_gain, ln_bias, qkv_weight.astype(jnp.float32), qv_bias, out_weight.astype(jnp.float32), out_bias, fc_weight.astype(jnp.float32), fc_bias, proj_weight.astype(jnp.float32), proj_bias)

    def run_section(inputs, *params):
        return jnp.stack([layer(inputs[batch_index], positions[batch_index], *params) for batch_index in range(MICRO)])
    first_out, first_back = jax.vjp(run_section, tokens.astype(jnp.float32), *[member[0] for member in weights])
    second_out, second_back = jax.vjp(run_section, low(first_out), *[member[1] for member in weights])
    second_grads = second_back(cotangent.astype(jnp.float32))
    first_grads = first_back(low(second_grads[0]))
    stacked = [jnp.stack([early, late]) for early, late in zip(first_grads[1:], second_grads[1:])]
    return (jnp.stack([first_out, second_out]).astype(jnp.bfloat16), jnp.stack([first_grads[0], second_grads[0]]), stacked[0], stacked[1], stacked[2], stacked[3], stacked[4], stacked[5], stacked[6], stacked[7], stacked[8], stacked[9])
```

```python
import functools
import math

import jax
import jax.numpy as jnp
from jax import lax
from jax.experimental import pallas as pl
from jax.experimental.pallas import tpu as pltpu
from jax.sharding import PartitionSpec as P

HEAD = 64


EPSILON = 1e-05
MASKED = -1e30
GELU_RATE = 0.7978845608028654
GELU_CUBE = 0.044715
MESH = pl.DeviceIdType.MESH
VMEM_BYTES = 48 * 1024 * 1024


def passed_along(block, axis, distance):
    devices = range(lax.axis_size(axis))
    route = [(i - distance, i) for i in devices if i - distance in devices]
    return lax.ppermute(block, axis, route)


def layer_norm(values, gains, biases):
    average = jnp.mean(values, axis=-1, keepdims=True)
    centered = values - average
    spread = jnp.mean(centered * centered, axis=-1, keepdims=True)
    return centered * lax.rsqrt(spread + EPSILON) * gains + biases


def gelu_tanh(values):
    return (
        0.5 * values * (1.0 + jnp.tanh(GELU_RATE * (values + GELU_CUBE * values * values * values)))
    )


def contract_rows(left, right):
    return lax.dot_general(
        left, right, (((0,), (0,)), ((), ())), preferred_element_type=jnp.float32
    )


def contract_cols(left, right):
    return lax.dot_general(
        left, right, (((1,), (1,)), ((), ())), preferred_element_type=jnp.float32
    )


def meet(axis, partners):
    barrier = pltpu.get_barrier_semaphore()
    for partner in partners:
        pl.semaphore_signal(barrier, inc=1, device_id={axis: partner}, device_id_type=MESH)
    pl.semaphore_wait(barrier, len(partners))


def meet_line(axis, me, count):
    barrier = pltpu.get_barrier_semaphore()

    @pl.when(me > 0)
    def _():
        pl.semaphore_signal(barrier, inc=1, device_id={axis: me - 1}, device_id_type=MESH)

    @pl.when(me < count - 1)
    def _():
        pl.semaphore_signal(barrier, inc=1, device_id={axis: me + 1}, device_id_type=MESH)

    neighbours = (me > 0).astype(jnp.int32) + (me < count - 1).astype(jnp.int32)
    pl.semaphore_wait(barrier, neighbours)


def sum_tensor_kernel(pieces, x_ref, o_ref, away, first, mine, second, last, send, recv):
    me = lax.axis_index("tensor")
    parity = lax.rem(me, 2)
    near = me + 1 - 2 * parity
    far = lax.rem(me + 2, 4)
    half = x_ref.shape[0] // 2
    rows = half // pieces
    meet("tensor", (near, far))

    def copy(source, target, step, k, device):
        span = pl.ds(k * rows, rows)
        return pltpu.make_async_remote_copy(
            src_ref=source.at[span],
            dst_ref=target.at[span],
            send_sem=send.at[step, k],
            recv_sem=recv.at[step, k],
            device_id={"tensor": device},
            device_id_type=MESH,
        )

    copies = [[None] * pieces for _ in range(3)]
    for k in range(pieces):
        span = pl.ds(k * rows, rows)
        begin = pl.multiple_of((1 - parity) * half + k * rows, 16)
        away[span] = x_ref[pl.ds(begin, rows)].astype(jnp.bfloat16)
        copies[0][k] = copy(away, first, 0, k, near)
        copies[0][k].start()
    for k in range(pieces):
        span = pl.ds(k * rows, rows)
        begin = pl.multiple_of(parity * half + k * rows, 16)
        copies[0][k].wait_recv()
        mine[span] = (x_ref[pl.ds(begin, rows)] + first[span].astype(jnp.float32)).astype(
            jnp.bfloat16
        )
        copies[1][k] = copy(mine, second, 1, k, far)
        copies[1][k].start()
    for k in range(pieces):
        span = pl.ds(k * rows, rows)
        begin = pl.multiple_of(parity * half + k * rows, 16)
        copies[1][k].wait_recv()
        copies[0][k].wait_send()
        away[span] = (mine[span].astype(jnp.float32) + second[span].astype(jnp.float32)).astype(
            jnp.bfloat16
        )
        copies[2][k] = copy(away, last, 2, k, near)
        copies[2][k].start()
        o_ref[pl.ds(begin, rows)] = away[span].astype(jnp.float32)
    for k in range(pieces):
        span = pl.ds(k * rows, rows)
        begin = pl.multiple_of((1 - parity) * half + k * rows, 16)
        copies[2][k].wait_recv()
        o_ref[pl.ds(begin, rows)] = last[span].astype(jnp.float32)
    for k in range(pieces):
        copies[1][k].wait_send()
        copies[2][k].wait_send()


def sum_tensor(partial):
    rows, width = partial.shape
    if lax.axis_size("tensor") != 4 or rows % 96:
        return lax.psum(partial, "tensor")
    half = pltpu.VMEM((rows // 2, width), jnp.bfloat16)
    pieces = 3
    return pl.pallas_call(
        functools.partial(sum_tensor_kernel, pieces),
        out_shape=jax.ShapeDtypeStruct((rows, width), jnp.float32),
        in_specs=[pl.BlockSpec(memory_space=pltpu.VMEM)],
        out_specs=pl.BlockSpec(memory_space=pltpu.VMEM),
        scratch_shapes=[half] * 5
        + [pltpu.SemaphoreType.DMA((3, pieces)), pltpu.SemaphoreType.DMA((3, pieces))],
        compiler_params=pltpu.CompilerParams(
            collective_id=0, has_side_effects=True, vmem_limit_bytes=VMEM_BYTES
        ),
    )(partial)


def gather_kernel(count, x_ref, o_ref, send, recv):
    me = lax.axis_index("dp")
    batches = x_ref.shape[0]
    meet_line("dp", me, count)
    o_ref[me] = x_ref[...]

    def copy(side, step, m):
        owner = me - step if side == 0 else me + step
        return pltpu.make_async_remote_copy(
            src_ref=o_ref.at[owner, m],
            dst_ref=o_ref.at[owner, m],
            send_sem=send.at[side, step, m],
            recv_sem=recv.at[side, step, m],
            device_id={"dp": me + 1 if side == 0 else me - 1},
            device_id_type=MESH,
        )

    def arrival(side, step, m):
        owner = me - 1 - step if side == 0 else me + 1 + step
        return pltpu.make_async_remote_copy(
            src_ref=o_ref.at[owner, m],
            dst_ref=o_ref.at[owner, m],
            send_sem=send.at[side, step, m],
            recv_sem=recv.at[side, step, m],
            device_id={"dp": me - 1 if side == 0 else me + 1},
            device_id_type=MESH,
        )

    def sends(side, step):
        if side == 0:
            return jnp.logical_and(me < count - 1, me - step >= 0)
        return jnp.logical_and(me > 0, me + step <= count - 1)

    def arrives(side, step):
        return me - 1 - step >= 0 if side == 0 else me + 1 + step <= count - 1

    for step in range(count - 1):
        for m in range(batches):
            for side in range(2):
                if step:

                    @pl.when(arrives(side, step - 1))
                    def _():
                        arrival(side, step - 1, m).wait_recv()

                @pl.when(sends(side, step))
                def _():
                    copy(side, step, m).start()

    for m in range(batches):
        for side in range(2):

            @pl.when(arrives(side, count - 2))
            def _():
                arrival(side, count - 2, m).wait_recv()

    for step in range(count - 1):
        for m in range(batches):
            for side in range(2):

                @pl.when(sends(side, step))
                def _():
                    copy(side, step, m).wait_send()


def gather_dp(block):
    count = lax.axis_size("dp")
    batches = block.shape[0]
    if count == 1:
        return block[None]
    semaphores = pltpu.SemaphoreType.DMA((2, count - 1, batches))
    return pl.pallas_call(
        functools.partial(gather_kernel, count),
        out_shape=jax.ShapeDtypeStruct((count,) + block.shape, block.dtype),
        in_specs=[pl.BlockSpec(memory_space=pltpu.VMEM)],
        out_specs=pl.BlockSpec(memory_space=pltpu.VMEM),
        scratch_shapes=[semaphores, semaphores],
        compiler_params=pltpu.CompilerParams(
            collective_id=1, has_side_effects=True, vmem_limit_bytes=VMEM_BYTES
        ),
    )(block)


def scatter_kernel(count, x_ref, o_ref, landed, send, recv):
    me = lax.axis_index("dp")
    batches = x_ref.shape[1]
    meet_line("dp", me, count)

    def copy(side, step, m, source):
        return pltpu.make_async_remote_copy(
            src_ref=source,
            dst_ref=landed.at[side, step, m],
            send_sem=send.at[side, step, m],
            recv_sem=recv.at[side, step, m],
            device_id={"dp": me + 1 if side == 0 else me - 1},
            device_id_type=MESH,
        )

    for step in range(count - 1):
        for m in range(batches):
            for side in range(2):
                owner = count - 1 - step if side == 0 else step
                at_end = me == 0 if side == 0 else me == count - 1
                inside = (
                    jnp.logical_and(me > 0, me < owner)
                    if side == 0
                    else jnp.logical_and(me < count - 1, me > owner)
                )

                @pl.when(at_end)
                def _():
                    copy(side, step, m, x_ref.at[owner, m]).start()

                @pl.when(inside)
                def _():
                    copy(side, step, m, landed.at[side, step, m]).wait_recv()
                    landed[side, step, m] = (
                        landed[side, step, m].astype(jnp.float32)
                        + x_ref[owner, m].astype(jnp.float32)
                    ).astype(jnp.bfloat16)
                    copy(side, step, m, landed.at[side, step, m]).start()

    for m in range(batches):
        o_ref[m] = x_ref[me, m].astype(jnp.float32)
        for side in range(2):
            step = count - 1 - me if side == 0 else me

            @pl.when(me > 0 if side == 0 else me < count - 1)
            def _():
                copy(side, step, m, landed.at[side, step, m]).wait_recv()
                o_ref[m] += landed[side, step, m].astype(jnp.float32)

    for step in range(count - 1):
        for m in range(batches):
            for side in range(2):
                owner = count - 1 - step if side == 0 else step

                @pl.when(me < owner if side == 0 else me > owner)
                def _():
                    copy(side, step, m, x_ref.at[owner, m]).wait_send()


def scatter_dp(terms):
    count, batches, rows, width = terms.shape
    if count == 1:
        return terms[0].astype(jnp.float32)
    semaphores = pltpu.SemaphoreType.DMA((2, count - 1, batches))
    return pl.pallas_call(
        functools.partial(scatter_kernel, count),
        out_shape=jax.ShapeDtypeStruct((batches, rows, width), jnp.float32),
        in_specs=[pl.BlockSpec(memory_space=pltpu.VMEM)],
        out_specs=pl.BlockSpec(memory_space=pltpu.VMEM),
        scratch_shapes=[
            pltpu.VMEM((2, count - 1, batches, rows, width), jnp.bfloat16),
            semaphores,
            semaphores,
        ],
        compiler_params=pltpu.CompilerParams(
            collective_id=2, has_side_effects=True, vmem_limit_bytes=VMEM_BYTES
        ),
    )(terms.astype(jnp.bfloat16))


def layer_forward(inputs, allowed, params):
    (
        gains,
        biases,
        qkv_weight,
        qv_bias,
        out_weight,
        out_bias,
        fc_weight,
        fc_bias,
        proj_weight,
        proj_bias,
    ) = params
    batches, _, shard_rows, key_count = allowed.shape
    local_width = qkv_weight.shape[2]
    head_count = local_width // HEAD
    normed = layer_norm(inputs, gains[0], biases[0]).astype(jnp.bfloat16)
    projected = jnp.dot(
        normed,
        qkv_weight.reshape(qkv_weight.shape[0], 3 * local_width),
        preferred_element_type=jnp.float32,
    )
    query = (projected[:, :local_width] + qv_bias[0]).astype(jnp.bfloat16)
    keys = projected[:, local_width : 2 * local_width].astype(jnp.bfloat16)
    values = (projected[:, 2 * local_width :] + qv_bias[1]).astype(jnp.bfloat16)
    pair = jnp.concatenate([keys, values], axis=1).reshape(batches, shard_rows, 2 * local_width)
    gathered = gather_dp(pair)
    gathered = gathered.transpose(1, 0, 2, 3).reshape(batches, key_count, 2, head_count, HEAD)
    key_heads = gathered[:, :, 0]
    value_heads = gathered[:, :, 1]
    queries = query.reshape(batches, shard_rows, head_count, HEAD)
    scores = jnp.einsum(
        "mqhe,mkhe->mhqk", queries, key_heads, preferred_element_type=jnp.float32
    ) * (1.0 / math.sqrt(HEAD))
    scores = jnp.where(allowed, scores, MASKED)
    peak = jnp.max(scores, axis=-1, keepdims=True)
    powers = jnp.where(allowed, jnp.exp(scores - peak), 0.0)
    softmax = powers / jnp.sum(powers, axis=-1, keepdims=True)
    attended = jnp.einsum(
        "mhqk,mkhe->mqhe",
        softmax.astype(jnp.bfloat16),
        value_heads,
        preferred_element_type=jnp.float32,
    )
    attended = attended.reshape(batches * shard_rows, local_width).astype(jnp.bfloat16)
    middle = (
        inputs
        + sum_tensor(jnp.dot(attended, out_weight, preferred_element_type=jnp.float32))
        + out_bias
    )
    normed_mid = layer_norm(middle, gains[1], biases[1]).astype(jnp.bfloat16)
    hidden_pre = jnp.dot(normed_mid, fc_weight, preferred_element_type=jnp.float32) + fc_bias
    active = gelu_tanh(hidden_pre).astype(jnp.bfloat16)
    output = (
        middle
        + sum_tensor(jnp.dot(active, proj_weight, preferred_element_type=jnp.float32))
        + proj_bias
    )
    saved_state = (
        inputs,
        normed,
        queries,
        key_heads,
        value_heads,
        softmax,
        attended,
        middle,
        normed_mid,
        hidden_pre,
        active,
    )
    return (output, saved_state)


def layer_backward(grad_output, saved_state, params, with_grads):
    (
        gains,
        biases,
        qkv_weight,
        qv_bias,
        out_weight,
        out_bias,
        fc_weight,
        fc_bias,
        proj_weight,
        proj_bias,
    ) = params
    (
        inputs,
        normed,
        queries,
        key_heads,
        value_heads,
        softmax,
        attended,
        middle,
        normed_mid,
        hidden_pre,
        active,
    ) = saved_state
    batches, shard_rows, head_count, _ = queries.shape
    rows = batches * shard_rows
    local_width = head_count * HEAD
    key_count = key_heads.shape[1]
    score_scale = 1.0 / math.sqrt(HEAD)

    def summed(member):
        return lax.psum(member.astype(jnp.bfloat16), "dp").astype(jnp.float32)

    grad_low = grad_output.astype(jnp.bfloat16)
    grad_active = contract_cols(grad_low, proj_weight)
    grad_pre = jax.vjp(gelu_tanh, hidden_pre)[1](grad_active)[0].astype(jnp.bfloat16)
    grad_normed_mid = sum_tensor(contract_cols(grad_pre, fc_weight))
    if with_grads:
        grad_proj_weight = summed(contract_rows(active, grad_low))
        grad_fc_weight = summed(contract_rows(normed_mid, grad_pre))
    grad_middle_norm, grad_gain_mid, grad_bias_mid = jax.vjp(
        layer_norm, middle, gains[1], biases[1]
    )[1](grad_normed_mid)
    grad_middle = grad_output + grad_middle_norm
    middle_low = grad_middle.astype(jnp.bfloat16)
    grad_attended = contract_cols(middle_low, out_weight).astype(jnp.bfloat16)
    if with_grads:
        grad_out_weight = summed(contract_rows(attended, middle_low))
    grad_heads = grad_attended.reshape(batches, shard_rows, head_count, HEAD)
    grad_softmax = jnp.einsum(
        "mqhe,mkhe->mhqk", grad_heads, value_heads, preferred_element_type=jnp.float32
    )
    delta = jnp.sum(softmax * grad_softmax, axis=-1, keepdims=True)
    grad_scores = (softmax * (grad_softmax - delta)).astype(jnp.bfloat16)
    grad_query = (
        jnp.einsum("mhqk,mkhe->mqhe", grad_scores, key_heads, preferred_element_type=jnp.float32)
        * score_scale
    )
    grad_keys = (
        jnp.einsum("mhqk,mqhe->mkhe", grad_scores, queries, preferred_element_type=jnp.float32)
        * score_scale
    )
    grad_values = jnp.einsum(
        "mhqk,mqhe->mkhe",
        softmax.astype(jnp.bfloat16),
        grad_heads,
        preferred_element_type=jnp.float32,
    )
    terms = jnp.concatenate(
        [
            grad_keys.reshape(batches, key_count, local_width),
            grad_values.reshape(batches, key_count, local_width),
        ],
        axis=2,
    ).astype(jnp.bfloat16)
    terms = terms.reshape(batches, key_count // shard_rows, shard_rows, 2 * local_width)
    key_grads = scatter_dp(terms.transpose(1, 0, 2, 3)).reshape(rows, 2 * local_width)
    grad_query = grad_query.reshape(rows, local_width).astype(jnp.bfloat16)
    grad_keys = key_grads[:, :local_width].astype(jnp.bfloat16)
    grad_values = key_grads[:, local_width:].astype(jnp.bfloat16)
    grad_projected = jnp.concatenate([grad_query, grad_keys, grad_values], axis=1)
    qkv_flat = qkv_weight.reshape(qkv_weight.shape[0], -1)
    if with_grads:
        grad_qkv_weight = summed(contract_rows(normed, grad_projected)).reshape(qkv_weight.shape)
    grad_normed = sum_tensor(contract_cols(grad_projected, qkv_flat))
    grad_input_norm, grad_gain_in, grad_bias_in = jax.vjp(layer_norm, inputs, gains[0], biases[0])[
        1
    ](grad_normed)
    grad_input = grad_middle + grad_input_norm
    if not with_grads:
        return (grad_input, None)
    small = jnp.concatenate(
        [
            grad_gain_in,
            grad_gain_mid,
            grad_bias_in,
            grad_bias_mid,
            jnp.sum(grad_query.astype(jnp.float32), axis=0),
            jnp.sum(grad_values.astype(jnp.float32), axis=0),
            jnp.sum(grad_middle, axis=0),
            jnp.sum(grad_pre.astype(jnp.float32), axis=0),
            jnp.sum(grad_output, axis=0),
        ]
    )
    small = lax.psum(small, "dp")
    width = gains.shape[1]
    sizes = (2 * width, 2 * width, 2 * local_width, width, fc_bias.shape[0], width)
    parts = []
    begin = 0
    for size in sizes:
        parts.append(small[begin : begin + size])
        begin += size
    grads = (
        parts[0].reshape(gains.shape),
        parts[1].reshape(biases.shape),
        grad_qkv_weight,
        parts[2].reshape(qv_bias.shape),
        grad_out_weight,
        parts[3],
        grad_fc_weight,
        parts[4],
        grad_proj_weight,
        parts[5],
    )
    return (grad_input, grads)


def per_device(
    tokens,
    block_order,
    ln_gain,
    ln_bias,
    qkv_weight,
    qv_bias,
    out_weight,
    out_bias,
    fc_weight,
    fc_bias,
    proj_weight,
    proj_bias,
    cotangent,
):
    micro_count, shard_rows, model_width = tokens.shape
    is_first = lax.axis_index("section") == 0
    dp_index = lax.axis_index("dp")
    params = (
        ln_gain[0],
        ln_bias[0],
        qkv_weight[0],
        qv_bias[0],
        out_weight[0],
        out_bias[0],
        fc_weight[0],
        fc_bias[0],
        proj_weight[0],
        proj_bias[0],
    )
    row_offsets = jnp.arange(shard_rows, dtype=jnp.int32)
    positions = block_order[:, :, None] * shard_rows + row_offsets
    key_pos = positions.reshape(micro_count, -1)
    query_pos = block_order[:, dp_index][:, None] * shard_rows + row_offsets
    allowed = (query_pos[:, :, None] >= key_pos[:, None, :])[:, None]
    rows = micro_count * shard_rows
    inputs = tokens.reshape(rows, model_width).astype(jnp.float32)
    output, _ = layer_forward(inputs, allowed, params)
    received = passed_along(output.astype(jnp.bfloat16), "section", 1).astype(jnp.float32)
    inputs = jnp.where(is_first, inputs, received)
    output, saved_state = layer_forward(inputs, allowed, params)
    seed_grad = cotangent.reshape(rows, model_width).astype(jnp.float32)
    grad_input, _ = layer_backward(seed_grad, saved_state, params, False)
    received = passed_along(grad_input.astype(jnp.bfloat16), "section", -1).astype(jnp.float32)
    grad_output = jnp.where(is_first, received, seed_grad)
    grad_input, grads = layer_backward(grad_output, saved_state, params, True)
    section_out = output.astype(jnp.bfloat16).reshape(tokens.shape)[None]
    section_grad = grad_input.reshape(tokens.shape)[None]
    return (section_out, section_grad) + tuple((member[None] for member in grads))


def solution(mesh):
    return jax.shard_map(
        per_device,
        mesh=mesh,
        in_specs=(
            P(None, "dp", None),
            P(),
            P("section", None, None),
            P("section", None, None),
            P("section", None, None, "tensor"),
            P("section", None, "tensor"),
            P("section", "tensor", None),
            P("section", None),
            P("section", None, "tensor"),
            P("section", "tensor"),
            P("section", "tensor", None),
            P("section", None),
            P(None, "dp", None),
        ),
        out_specs=(
            P("section", None, "dp", None),
            P("section", None, "dp", None),
            P("section", None, None),
            P("section", None, None),
            P("section", None, None, "tensor"),
            P("section", None, "tensor"),
            P("section", "tensor", None),
            P("section", None),
            P("section", None, "tensor"),
            P("section", "tensor"),
            P("section", "tensor", None),
            P("section", None),
        ),
        check_vma=False,
    )
```

```python
import functools
import math

import jax
import jax.numpy as jnp
from jax import lax
from jax.experimental import pallas as pl
from jax.experimental.pallas import tpu as pltpu
from jax.sharding import PartitionSpec as P

HEAD = 64


EPSILON = 1e-05
MASKED = -1e30
GELU_RATE = 0.7978845608028654
GELU_CUBE = 0.044715
MESH = pl.DeviceIdType.MESH
VMEM_BYTES = 48 * 1024 * 1024


def layer_norm(values, gains, biases):
    average = jnp.mean(values, axis=-1, keepdims=True)
    centered = values - average
    spread = jnp.mean(centered * centered, axis=-1, keepdims=True)
    return centered * lax.rsqrt(spread + EPSILON) * gains + biases


def gelu_tanh(values):
    return (
        0.5 * values * (1.0 + jnp.tanh(GELU_RATE * (values + GELU_CUBE * values * values * values)))
    )


def contract_rows(left, right):
    return lax.dot_general(
        left, right, (((0,), (0,)), ((), ())), preferred_element_type=jnp.float32
    )


def contract_cols(left, right):
    return lax.dot_general(
        left, right, (((1,), (1,)), ((), ())), preferred_element_type=jnp.float32
    )


def meet(axis, partners):
    barrier = pltpu.get_barrier_semaphore()
    for partner in partners:
        pl.semaphore_signal(barrier, inc=1, device_id={axis: partner}, device_id_type=MESH)
    pl.semaphore_wait(barrier, len(partners))


def meet_line(axis, me, count):
    barrier = pltpu.get_barrier_semaphore()

    @pl.when(me > 0)
    def _():
        pl.semaphore_signal(barrier, inc=1, device_id={axis: me - 1}, device_id_type=MESH)

    @pl.when(me < count - 1)
    def _():
        pl.semaphore_signal(barrier, inc=1, device_id={axis: me + 1}, device_id_type=MESH)

    neighbours = (me > 0).astype(jnp.int32) + (me < count - 1).astype(jnp.int32)
    pl.semaphore_wait(barrier, neighbours)


def sum_tensor_kernel(pieces, x_ref, o_ref, away, first, mine, second, last, send, recv):
    me = lax.axis_index("tensor")
    parity = lax.rem(me, 2)
    near = me + 1 - 2 * parity
    far = lax.rem(me + 2, 4)
    half = x_ref.shape[0] // 2
    rows = half // pieces
    meet("tensor", (near, far))

    def copy(source, target, step, k, device):
        span = pl.ds(k * rows, rows)
        return pltpu.make_async_remote_copy(
            src_ref=source.at[span],
            dst_ref=target.at[span],
            send_sem=send.at[step, k],
            recv_sem=recv.at[step, k],
            device_id={"tensor": device},
            device_id_type=MESH,
        )

    copies = [[None] * pieces for _ in range(3)]
    for k in range(pieces):
        span = pl.ds(k * rows, rows)
        begin = pl.multiple_of((1 - parity) * half + k * rows, 16)
        away[span] = x_ref[pl.ds(begin, rows)].astype(jnp.bfloat16)
        copies[0][k] = copy(away, first, 0, k, near)
        copies[0][k].start()
    for k in range(pieces):
        span = pl.ds(k * rows, rows)
        begin = pl.multiple_of(parity * half + k * rows, 16)
        copies[0][k].wait_recv()
        mine[span] = (x_ref[pl.ds(begin, rows)] + first[span].astype(jnp.float32)).astype(
            jnp.bfloat16
        )
        copies[1][k] = copy(mine, second, 1, k, far)
        copies[1][k].start()
    for k in range(pieces):
        span = pl.ds(k * rows, rows)
        begin = pl.multiple_of(parity * half + k * rows, 16)
        copies[1][k].wait_recv()
        copies[0][k].wait_send()
        away[span] = (mine[span].astype(jnp.float32) + second[span].astype(jnp.float32)).astype(
            jnp.bfloat16
        )
        copies[2][k] = copy(away, last, 2, k, near)
        copies[2][k].start()
        o_ref[pl.ds(begin, rows)] = away[span].astype(jnp.float32)
    for k in range(pieces):
        span = pl.ds(k * rows, rows)
        begin = pl.multiple_of((1 - parity) * half + k * rows, 16)
        copies[2][k].wait_recv()
        o_ref[pl.ds(begin, rows)] = last[span].astype(jnp.float32)
    for k in range(pieces):
        copies[1][k].wait_send()
        copies[2][k].wait_send()


def sum_tensor(partial):
    rows, width = partial.shape
    if lax.axis_size("tensor") != 4 or rows % 96:
        return lax.psum(partial, "tensor")
    half = pltpu.VMEM((rows // 2, width), jnp.bfloat16)
    pieces = 3
    return pl.pallas_call(
        functools.partial(sum_tensor_kernel, pieces),
        out_shape=jax.ShapeDtypeStruct((rows, width), jnp.float32),
        in_specs=[pl.BlockSpec(memory_space=pltpu.VMEM)],
        out_specs=pl.BlockSpec(memory_space=pltpu.VMEM),
        scratch_shapes=[half] * 5
        + [pltpu.SemaphoreType.DMA((3, pieces)), pltpu.SemaphoreType.DMA((3, pieces))],
        compiler_params=pltpu.CompilerParams(
            collective_id=0, has_side_effects=True, vmem_limit_bytes=VMEM_BYTES
        ),
    )(partial)


def swap_kernel(pieces, x_ref, o_ref, send, recv):
    section = lax.axis_index("section")
    me = lax.axis_index("tensor")
    parity = lax.rem(me, 2)
    near = me + 1 - 2 * parity
    half = x_ref.shape[0] // 2
    rows = half // pieces
    barrier = pltpu.get_barrier_semaphore()
    pl.semaphore_signal(
        barrier, inc=1, device_id={"section": 1 - section}, device_id_type=MESH
    )
    pl.semaphore_signal(barrier, inc=1, device_id={"tensor": near}, device_id_type=MESH)
    pl.semaphore_wait(barrier, 2)

    def copy(source, step, k, owner, device):
        span = pl.ds(pl.multiple_of(owner * half + k * rows, 16), rows)
        return pltpu.make_async_remote_copy(
            src_ref=source.at[span],
            dst_ref=o_ref.at[span],
            send_sem=send.at[step, k],
            recv_sem=recv.at[step, k],
            device_id=device,
            device_id_type=MESH,
        )

    across = [copy(x_ref, 0, k, parity, {"section": 1 - section}) for k in range(pieces)]
    beside = [copy(o_ref, 1, k, parity, {"tensor": near}) for k in range(pieces)]
    arriving = [copy(o_ref, 1, k, 1 - parity, {"tensor": near}) for k in range(pieces)]
    for k in range(pieces):
        across[k].start()
    for k in range(pieces):
        across[k].wait_recv()
        beside[k].start()
    for k in range(pieces):
        arriving[k].wait_recv()
        across[k].wait_send()
        beside[k].wait_send()


def swap_sections(block):
    pieces = 3
    if lax.axis_size("section") != 2 or lax.axis_size("tensor") % 2 or block.shape[0] % 96:
        return lax.ppermute(block, "section", [(0, 1), (1, 0)])
    return pl.pallas_call(
        functools.partial(swap_kernel, pieces),
        out_shape=jax.ShapeDtypeStruct(block.shape, block.dtype),
        in_specs=[pl.BlockSpec(memory_space=pltpu.VMEM)],
        out_specs=pl.BlockSpec(memory_space=pltpu.VMEM),
        scratch_shapes=[
            pltpu.SemaphoreType.DMA((2, pieces)),
            pltpu.SemaphoreType.DMA((2, pieces)),
        ],
        compiler_params=pltpu.CompilerParams(
            collective_id=3, has_side_effects=True, vmem_limit_bytes=VMEM_BYTES
        ),
    )(block)


def gather_kernel(count, x_ref, o_ref, send, recv):
    me = lax.axis_index("dp")
    batches = x_ref.shape[0]
    meet_line("dp", me, count)
    o_ref[me] = x_ref[...]

    def copy(side, step, m):
        owner = me - step if side == 0 else me + step
        return pltpu.make_async_remote_copy(
            src_ref=o_ref.at[owner, m],
            dst_ref=o_ref.at[owner, m],
            send_sem=send.at[side, step, m],
            recv_sem=recv.at[side, step, m],
            device_id={"dp": me + 1 if side == 0 else me - 1},
            device_id_type=MESH,
        )

    def arrival(side, step, m):
        owner = me - 1 - step if side == 0 else me + 1 + step
        return pltpu.make_async_remote_copy(
            src_ref=o_ref.at[owner, m],
            dst_ref=o_ref.at[owner, m],
            send_sem=send.at[side, step, m],
            recv_sem=recv.at[side, step, m],
            device_id={"dp": me - 1 if side == 0 else me + 1},
            device_id_type=MESH,
        )

    def sends(side, step):
        if side == 0:
            return jnp.logical_and(me < count - 1, me - step >= 0)
        return jnp.logical_and(me > 0, me + step <= count - 1)

    def arrives(side, step):
        return me - 1 - step >= 0 if side == 0 else me + 1 + step <= count - 1

    for step in range(count - 1):
        for m in range(batches):
            for side in range(2):
                if step:

                    @pl.when(arrives(side, step - 1))
                    def _():
                        arrival(side, step - 1, m).wait_recv()

                @pl.when(sends(side, step))
                def _():
                    copy(side, step, m).start()

    for m in range(batches):
        for side in range(2):

            @pl.when(arrives(side, count - 2))
            def _():
                arrival(side, count - 2, m).wait_recv()

    for step in range(count - 1):
        for m in range(batches):
            for side in range(2):

                @pl.when(sends(side, step))
                def _():
                    copy(side, step, m).wait_send()


def gather_dp(block):
    count = lax.axis_size("dp")
    batches = block.shape[0]
    if count == 1:
        return block[None]
    semaphores = pltpu.SemaphoreType.DMA((2, count - 1, batches))
    return pl.pallas_call(
        functools.partial(gather_kernel, count),
        out_shape=jax.ShapeDtypeStruct((count,) + block.shape, block.dtype),
        in_specs=[pl.BlockSpec(memory_space=pltpu.VMEM)],
        out_specs=pl.BlockSpec(memory_space=pltpu.VMEM),
        scratch_shapes=[semaphores, semaphores],
        compiler_params=pltpu.CompilerParams(
            collective_id=1, has_side_effects=True, vmem_limit_bytes=VMEM_BYTES
        ),
    )(block)


def scatter_kernel(count, x_ref, o_ref, landed, send, recv):
    me = lax.axis_index("dp")
    batches = x_ref.shape[1]
    meet_line("dp", me, count)

    def copy(side, step, m, source):
        return pltpu.make_async_remote_copy(
            src_ref=source,
            dst_ref=landed.at[side, step, m],
            send_sem=send.at[side, step, m],
            recv_sem=recv.at[side, step, m],
            device_id={"dp": me + 1 if side == 0 else me - 1},
            device_id_type=MESH,
        )

    for step in range(count - 1):
        for m in range(batches):
            for side in range(2):
                owner = count - 1 - step if side == 0 else step

                @pl.when(me == 0 if side == 0 else me == count - 1)
                def _():
                    copy(side, step, m, x_ref.at[owner, m]).start()

    items = (count - 1) * batches
    for slot in range(1, items + count - 2):
        for side in range(2):
            item = slot - (me if side == 0 else count - 1 - me)
            step = lax.div(item, batches)
            m = item - step * batches
            owner = count - 1 - step if side == 0 else step
            moves = me < owner if side == 0 else me > owner
            inner = me > 0 if side == 0 else me < count - 1
            valid = jnp.logical_and(item >= 0, item < items)

            @pl.when(jnp.logical_and(jnp.logical_and(inner, valid), moves))
            def _():
                copy(side, step, m, landed.at[side, step, m]).wait_recv()
                landed[side, step, m] = (
                    landed[side, step, m].astype(jnp.float32)
                    + x_ref[owner, m].astype(jnp.float32)
                ).astype(jnp.bfloat16)
                copy(side, step, m, landed.at[side, step, m]).start()

    for m in range(batches):
        o_ref[m] = x_ref[me, m].astype(jnp.float32)
        for side in range(2):
            step = count - 1 - me if side == 0 else me

            @pl.when(me > 0 if side == 0 else me < count - 1)
            def _():
                copy(side, step, m, landed.at[side, step, m]).wait_recv()
                o_ref[m] += landed[side, step, m].astype(jnp.float32)

    for step in range(count - 1):
        for m in range(batches):
            for side in range(2):
                owner = count - 1 - step if side == 0 else step

                @pl.when(me < owner if side == 0 else me > owner)
                def _():
                    copy(side, step, m, x_ref.at[owner, m]).wait_send()


def scatter_dp(terms):
    count, batches, rows, width = terms.shape
    if count == 1:
        return terms[0].astype(jnp.float32)
    semaphores = pltpu.SemaphoreType.DMA((2, count - 1, batches))
    return pl.pallas_call(
        functools.partial(scatter_kernel, count),
        out_shape=jax.ShapeDtypeStruct((batches, rows, width), jnp.float32),
        in_specs=[pl.BlockSpec(memory_space=pltpu.VMEM)],
        out_specs=pl.BlockSpec(memory_space=pltpu.VMEM),
        scratch_shapes=[
            pltpu.VMEM((2, count - 1, batches, rows, width), jnp.bfloat16),
            semaphores,
            semaphores,
        ],
        compiler_params=pltpu.CompilerParams(
            collective_id=2, has_side_effects=True, vmem_limit_bytes=VMEM_BYTES
        ),
    )(terms.astype(jnp.bfloat16))


def layer_forward(inputs, allowed, params):
    (
        gains,
        biases,
        qkv_weight,
        qv_bias,
        out_weight,
        out_bias,
        fc_weight,
        fc_bias,
        proj_weight,
        proj_bias,
    ) = params
    batches, _, shard_rows, key_count = allowed.shape
    local_width = qkv_weight.shape[2]
    head_count = local_width // HEAD
    normed = layer_norm(inputs, gains[0], biases[0]).astype(jnp.bfloat16)
    projected = jnp.dot(
        normed,
        qkv_weight.reshape(qkv_weight.shape[0], 3 * local_width),
        preferred_element_type=jnp.float32,
    )
    query = (projected[:, :local_width] + qv_bias[0]).astype(jnp.bfloat16)
    keys = projected[:, local_width : 2 * local_width].astype(jnp.bfloat16)
    values = (projected[:, 2 * local_width :] + qv_bias[1]).astype(jnp.bfloat16)
    pair = jnp.concatenate([keys, values], axis=1).reshape(batches, shard_rows, 2 * local_width)
    gathered = gather_dp(pair)
    gathered = gathered.transpose(1, 0, 2, 3).reshape(batches, key_count, 2, head_count, HEAD)
    key_heads = gathered[:, :, 0]
    value_heads = gathered[:, :, 1]
    queries = query.reshape(batches, shard_rows, head_count, HEAD)
    scores = jnp.einsum(
        "mqhe,mkhe->mhqk", queries, key_heads, preferred_element_type=jnp.float32
    ) * (1.0 / math.sqrt(HEAD))
    scores = jnp.where(allowed, scores, MASKED)
    peak = jnp.max(scores, axis=-1, keepdims=True)
    powers = jnp.where(allowed, jnp.exp(scores - peak), 0.0)
    softmax = powers / jnp.sum(powers, axis=-1, keepdims=True)
    attended = jnp.einsum(
        "mhqk,mkhe->mqhe",
        softmax.astype(jnp.bfloat16),
        value_heads,
        preferred_element_type=jnp.float32,
    )
    attended = attended.reshape(batches * shard_rows, local_width).astype(jnp.bfloat16)
    middle = (
        inputs
        + sum_tensor(jnp.dot(attended, out_weight, preferred_element_type=jnp.float32))
        + out_bias
    )
    normed_mid = layer_norm(middle, gains[1], biases[1]).astype(jnp.bfloat16)
    hidden_pre = jnp.dot(normed_mid, fc_weight, preferred_element_type=jnp.float32) + fc_bias
    active = gelu_tanh(hidden_pre).astype(jnp.bfloat16)
    output = (
        middle
        + sum_tensor(jnp.dot(active, proj_weight, preferred_element_type=jnp.float32))
        + proj_bias
    )
    saved_state = (
        inputs,
        normed,
        queries,
        key_heads,
        value_heads,
        softmax,
        attended,
        middle,
        normed_mid,
        hidden_pre,
        active,
    )
    return (output, saved_state)


def layer_backward(grad_output, saved_state, params, with_grads):
    (
        gains,
        biases,
        qkv_weight,
        qv_bias,
        out_weight,
        out_bias,
        fc_weight,
        fc_bias,
        proj_weight,
        proj_bias,
    ) = params
    (
        inputs,
        normed,
        queries,
        key_heads,
        value_heads,
        softmax,
        attended,
        middle,
        normed_mid,
        hidden_pre,
        active,
    ) = saved_state
    batches, shard_rows, head_count, _ = queries.shape
    rows = batches * shard_rows
    local_width = head_count * HEAD
    key_count = key_heads.shape[1]
    score_scale = 1.0 / math.sqrt(HEAD)

    grad_low = grad_output.astype(jnp.bfloat16)
    grad_active = contract_cols(grad_low, proj_weight)
    grad_pre = jax.vjp(gelu_tanh, hidden_pre)[1](grad_active)[0].astype(jnp.bfloat16)
    grad_normed_mid = sum_tensor(contract_cols(grad_pre, fc_weight))
    if with_grads:
        grad_proj_weight = contract_rows(active, grad_low).astype(jnp.bfloat16)
        grad_fc_weight = contract_rows(normed_mid, grad_pre).astype(jnp.bfloat16)
    grad_middle_norm, grad_gain_mid, grad_bias_mid = jax.vjp(
        layer_norm, middle, gains[1], biases[1]
    )[1](grad_normed_mid)
    grad_middle = grad_output + grad_middle_norm
    middle_low = grad_middle.astype(jnp.bfloat16)
    grad_attended = contract_cols(middle_low, out_weight).astype(jnp.bfloat16)
    if with_grads:
        grad_out_weight = contract_rows(attended, middle_low).astype(jnp.bfloat16)
        early = lax.psum((grad_proj_weight, grad_fc_weight, grad_out_weight), "dp")
    grad_heads = grad_attended.reshape(batches, shard_rows, head_count, HEAD)
    grad_softmax = jnp.einsum(
        "mqhe,mkhe->mhqk", grad_heads, value_heads, preferred_element_type=jnp.float32
    )
    delta = jnp.sum(softmax * grad_softmax, axis=-1, keepdims=True)
    grad_scores = (softmax * (grad_softmax - delta)).astype(jnp.bfloat16)
    grad_query = (
        jnp.einsum("mhqk,mkhe->mqhe", grad_scores, key_heads, preferred_element_type=jnp.float32)
        * score_scale
    )
    grad_keys = (
        jnp.einsum("mhqk,mqhe->mkhe", grad_scores, queries, preferred_element_type=jnp.float32)
        * score_scale
    )
    grad_values = jnp.einsum(
        "mhqk,mqhe->mkhe",
        softmax.astype(jnp.bfloat16),
        grad_heads,
        preferred_element_type=jnp.float32,
    )
    terms = jnp.concatenate(
        [
            grad_keys.reshape(batches, key_count, local_width),
            grad_values.reshape(batches, key_count, local_width),
        ],
        axis=2,
    ).astype(jnp.bfloat16)
    terms = terms.reshape(batches, key_count // shard_rows, shard_rows, 2 * local_width)
    key_grads = scatter_dp(terms.transpose(1, 0, 2, 3)).reshape(rows, 2 * local_width)
    grad_query = grad_query.reshape(rows, local_width).astype(jnp.bfloat16)
    grad_keys = key_grads[:, :local_width].astype(jnp.bfloat16)
    grad_values = key_grads[:, local_width:].astype(jnp.bfloat16)
    grad_projected = jnp.concatenate([grad_query, grad_keys, grad_values], axis=1)
    qkv_flat = qkv_weight.reshape(qkv_weight.shape[0], -1)
    if with_grads:
        grad_qkv_weight = contract_rows(normed, grad_projected).astype(jnp.bfloat16)
    grad_normed = sum_tensor(contract_cols(grad_projected, qkv_flat))
    grad_input_norm, grad_gain_in, grad_bias_in = jax.vjp(layer_norm, inputs, gains[0], biases[0])[
        1
    ](grad_normed)
    grad_input = grad_middle + grad_input_norm
    if not with_grads:
        return (grad_input, None)
    small = jnp.concatenate(
        [
            grad_gain_in,
            grad_gain_mid,
            grad_bias_in,
            grad_bias_mid,
            jnp.sum(grad_query.astype(jnp.float32), axis=0),
            jnp.sum(grad_values.astype(jnp.float32), axis=0),
            jnp.sum(grad_middle, axis=0),
            jnp.sum(grad_pre.astype(jnp.float32), axis=0),
            jnp.sum(grad_output, axis=0),
        ]
    ).astype(jnp.bfloat16)
    columns = 3 * local_width
    small_rows = -(-small.shape[0] // columns)
    small = jnp.pad(small, (0, small_rows * columns - small.shape[0]))
    late = jnp.concatenate([grad_qkv_weight, small.reshape(small_rows, columns)], axis=0)
    late, early = lax.optimization_barrier((late, early))
    late = lax.psum(late, "dp").astype(jnp.float32)
    grad_proj_weight, grad_fc_weight, grad_out_weight = (
        member.astype(jnp.float32) for member in early
    )
    grad_qkv_weight = late[: qkv_weight.shape[0]]
    small = late[qkv_weight.shape[0] :].reshape(-1)
    width = gains.shape[1]
    sizes = (2 * width, 2 * width, 2 * local_width, width, fc_bias.shape[0], width)
    parts = []
    begin = 0
    for size in sizes:
        parts.append(small[begin : begin + size])
        begin += size
    grads = (
        parts[0].reshape(gains.shape),
        parts[1].reshape(biases.shape),
        grad_qkv_weight.reshape(qkv_weight.shape),
        parts[2].reshape(qv_bias.shape),
        grad_out_weight,
        parts[3],
        grad_fc_weight,
        parts[4],
        grad_proj_weight,
        parts[5],
    )
    return (grad_input, grads)


def per_device(
    tokens,
    block_order,
    ln_gain,
    ln_bias,
    qkv_weight,
    qv_bias,
    out_weight,
    out_bias,
    fc_weight,
    fc_bias,
    proj_weight,
    proj_bias,
    cotangent,
):
    micro_count, shard_rows, model_width = tokens.shape
    is_first = lax.axis_index("section") == 0
    dp_index = lax.axis_index("dp")
    params = (
        ln_gain[0],
        ln_bias[0],
        qkv_weight[0],
        qv_bias[0],
        out_weight[0],
        out_bias[0],
        fc_weight[0],
        fc_bias[0],
        proj_weight[0],
        proj_bias[0],
    )
    row_offsets = jnp.arange(shard_rows, dtype=jnp.int32)
    positions = block_order[:, :, None] * shard_rows + row_offsets
    key_pos = positions.reshape(micro_count, -1)
    query_pos = block_order[:, dp_index][:, None] * shard_rows + row_offsets
    allowed = (query_pos[:, :, None] >= key_pos[:, None, :])[:, None]
    rows = micro_count * shard_rows
    inputs = tokens.reshape(rows, model_width).astype(jnp.float32)
    output, _ = layer_forward(inputs, allowed, params)
    received = swap_sections(output.astype(jnp.bfloat16)).astype(jnp.float32)
    inputs = jnp.where(is_first, inputs, received)
    output, saved_state = layer_forward(inputs, allowed, params)
    seed_grad = cotangent.reshape(rows, model_width).astype(jnp.float32)
    grad_input, _ = layer_backward(seed_grad, saved_state, params, False)
    received = swap_sections(grad_input.astype(jnp.bfloat16)).astype(jnp.float32)
    grad_output = jnp.where(is_first, received, seed_grad)
    grad_input, grads = layer_backward(grad_output, saved_state, params, True)
    section_out = output.astype(jnp.bfloat16).reshape(tokens.shape)[None]
    section_grad = grad_input.reshape(tokens.shape)[None]
    return (section_out, section_grad) + tuple((member[None] for member in grads))


def solution(mesh):
    return jax.shard_map(
        per_device,
        mesh=mesh,
        in_specs=(
            P(None, "dp", None),
            P(),
            P("section", None, None),
            P("section", None, None),
            P("section", None, None, "tensor"),
            P("section", None, "tensor"),
            P("section", "tensor", None),
            P("section", None),
            P("section", None, "tensor"),
            P("section", "tensor"),
            P("section", "tensor", None),
            P("section", None),
            P(None, "dp", None),
        ),
        out_specs=(
            P("section", None, "dp", None),
            P("section", None, "dp", None),
            P("section", None, None),
            P("section", None, None),
            P("section", None, None, "tensor"),
            P("section", None, "tensor"),
            P("section", "tensor", None),
            P("section", None),
            P("section", None, "tensor"),
            P("section", "tensor"),
            P("section", "tensor", None),
            P("section", None),
        ),
        check_vma=False,
    )
```

```python
import functools
import math

import jax
import jax.numpy as jnp
from jax import lax
from jax.experimental import pallas as pl
from jax.experimental.pallas import tpu as pltpu
from jax.sharding import PartitionSpec as P

HEAD = 64


EPSILON = 1e-05
MASKED = -1e30
GELU_RATE = 0.7978845608028654
GELU_CUBE = 0.044715
MESH = pl.DeviceIdType.MESH
VMEM_BYTES = 48 * 1024 * 1024


def layer_norm(values, gains, biases):
    average = jnp.mean(values, axis=-1, keepdims=True)
    centered = values - average
    spread = jnp.mean(centered * centered, axis=-1, keepdims=True)
    return centered * lax.rsqrt(spread + EPSILON) * gains + biases


def gelu_tanh(values):
    return (
        0.5 * values * (1.0 + jnp.tanh(GELU_RATE * (values + GELU_CUBE * values * values * values)))
    )


def contract_rows(left, right):
    return lax.dot_general(
        left, right, (((0,), (0,)), ((), ())), preferred_element_type=jnp.float32
    )


def contract_cols(left, right):
    return lax.dot_general(
        left, right, (((1,), (1,)), ((), ())), preferred_element_type=jnp.float32
    )


def meet(axis, partners):
    barrier = pltpu.get_barrier_semaphore()
    for partner in partners:
        pl.semaphore_signal(barrier, inc=1, device_id={axis: partner}, device_id_type=MESH)
    pl.semaphore_wait(barrier, len(partners))


def meet_line(axis, me, count):
    barrier = pltpu.get_barrier_semaphore()

    @pl.when(me > 0)
    def _():
        pl.semaphore_signal(barrier, inc=1, device_id={axis: me - 1}, device_id_type=MESH)

    @pl.when(me < count - 1)
    def _():
        pl.semaphore_signal(barrier, inc=1, device_id={axis: me + 1}, device_id_type=MESH)

    neighbours = (me > 0).astype(jnp.int32) + (me < count - 1).astype(jnp.int32)
    pl.semaphore_wait(barrier, neighbours)


def sum_tensor_kernel(pieces, x_ref, o_ref, away, first, mine, second, last, send, recv):
    me = lax.axis_index("tensor")
    parity = lax.rem(me, 2)
    near = me + 1 - 2 * parity
    far = lax.rem(me + 2, 4)
    half = x_ref.shape[0] // 2
    rows = half // pieces
    meet("tensor", (near, far))

    def copy(source, target, step, k, device):
        span = pl.ds(k * rows, rows)
        return pltpu.make_async_remote_copy(
            src_ref=source.at[span],
            dst_ref=target.at[span],
            send_sem=send.at[step, k],
            recv_sem=recv.at[step, k],
            device_id={"tensor": device},
            device_id_type=MESH,
        )

    copies = [[None] * pieces for _ in range(3)]
    for k in range(pieces):
        span = pl.ds(k * rows, rows)
        begin = pl.multiple_of((1 - parity) * half + k * rows, 16)
        away[span] = x_ref[pl.ds(begin, rows)].astype(jnp.bfloat16)
        copies[0][k] = copy(away, first, 0, k, near)
        copies[0][k].start()
    for k in range(pieces):
        span = pl.ds(k * rows, rows)
        begin = pl.multiple_of(parity * half + k * rows, 16)
        copies[0][k].wait_recv()
        mine[span] = (x_ref[pl.ds(begin, rows)] + first[span].astype(jnp.float32)).astype(
            jnp.bfloat16
        )
        copies[1][k] = copy(mine, second, 1, k, far)
        copies[1][k].start()
    for k in range(pieces):
        span = pl.ds(k * rows, rows)
        begin = pl.multiple_of(parity * half + k * rows, 16)
        copies[1][k].wait_recv()
        copies[0][k].wait_send()
        away[span] = (mine[span].astype(jnp.float32) + second[span].astype(jnp.float32)).astype(
            jnp.bfloat16
        )
        copies[2][k] = copy(away, last, 2, k, near)
        copies[2][k].start()
        o_ref[pl.ds(begin, rows)] = away[span].astype(jnp.float32)
    for k in range(pieces):
        span = pl.ds(k * rows, rows)
        begin = pl.multiple_of((1 - parity) * half + k * rows, 16)
        copies[2][k].wait_recv()
        o_ref[pl.ds(begin, rows)] = last[span].astype(jnp.float32)
    for k in range(pieces):
        copies[1][k].wait_send()
        copies[2][k].wait_send()


def sum_tensor(partial):
    rows, width = partial.shape
    if lax.axis_size("tensor") != 4 or rows % 96:
        return lax.psum(partial, "tensor")
    half = pltpu.VMEM((rows // 2, width), jnp.bfloat16)
    pieces = 3
    return pl.pallas_call(
        functools.partial(sum_tensor_kernel, pieces),
        out_shape=jax.ShapeDtypeStruct((rows, width), jnp.float32),
        in_specs=[pl.BlockSpec(memory_space=pltpu.VMEM)],
        out_specs=pl.BlockSpec(memory_space=pltpu.VMEM),
        scratch_shapes=[half] * 5
        + [pltpu.SemaphoreType.DMA((3, pieces)), pltpu.SemaphoreType.DMA((3, pieces))],
        compiler_params=pltpu.CompilerParams(
            collective_id=0, has_side_effects=True, vmem_limit_bytes=VMEM_BYTES
        ),
    )(partial)


def swap_kernel(pieces, x_ref, o_ref, send, recv):
    section = lax.axis_index("section")
    me = lax.axis_index("tensor")
    parity = lax.rem(me, 2)
    near = me + 1 - 2 * parity
    half = x_ref.shape[0] // 2
    rows = half // pieces
    barrier = pltpu.get_barrier_semaphore()
    pl.semaphore_signal(
        barrier, inc=1, device_id={"section": 1 - section}, device_id_type=MESH
    )
    pl.semaphore_signal(barrier, inc=1, device_id={"tensor": near}, device_id_type=MESH)
    pl.semaphore_wait(barrier, 2)

    def copy(source, step, k, owner, device):
        span = pl.ds(pl.multiple_of(owner * half + k * rows, 16), rows)
        return pltpu.make_async_remote_copy(
            src_ref=source.at[span],
            dst_ref=o_ref.at[span],
            send_sem=send.at[step, k],
            recv_sem=recv.at[step, k],
            device_id=device,
            device_id_type=MESH,
        )

    across = [copy(x_ref, 0, k, parity, {"section": 1 - section}) for k in range(pieces)]
    beside = [copy(o_ref, 1, k, parity, {"tensor": near}) for k in range(pieces)]
    arriving = [copy(o_ref, 1, k, 1 - parity, {"tensor": near}) for k in range(pieces)]
    for k in range(pieces):
        across[k].start()
    for k in range(pieces):
        across[k].wait_recv()
        beside[k].start()
    for k in range(pieces):
        arriving[k].wait_recv()
        across[k].wait_send()
        beside[k].wait_send()


def swap_sections(block):
    pieces = 3
    if lax.axis_size("section") != 2 or lax.axis_size("tensor") % 2 or block.shape[0] % 96:
        return lax.ppermute(block, "section", [(0, 1), (1, 0)])
    return pl.pallas_call(
        functools.partial(swap_kernel, pieces),
        out_shape=jax.ShapeDtypeStruct(block.shape, block.dtype),
        in_specs=[pl.BlockSpec(memory_space=pltpu.VMEM)],
        out_specs=pl.BlockSpec(memory_space=pltpu.VMEM),
        scratch_shapes=[
            pltpu.SemaphoreType.DMA((2, pieces)),
            pltpu.SemaphoreType.DMA((2, pieces)),
        ],
        compiler_params=pltpu.CompilerParams(
            collective_id=3, has_side_effects=True, vmem_limit_bytes=VMEM_BYTES
        ),
    )(block)


def gather_kernel(count, x_ref, o_ref, send, recv):
    me = lax.axis_index("dp")
    batches = x_ref.shape[0]
    meet_line("dp", me, count)
    o_ref[me] = x_ref[...]

    def copy(side, step, m):
        owner = me - step if side == 0 else me + step
        return pltpu.make_async_remote_copy(
            src_ref=o_ref.at[owner, m],
            dst_ref=o_ref.at[owner, m],
            send_sem=send.at[side, step, m],
            recv_sem=recv.at[side, step, m],
            device_id={"dp": me + 1 if side == 0 else me - 1},
            device_id_type=MESH,
        )

    def arrival(side, step, m):
        owner = me - 1 - step if side == 0 else me + 1 + step
        return pltpu.make_async_remote_copy(
            src_ref=o_ref.at[owner, m],
            dst_ref=o_ref.at[owner, m],
            send_sem=send.at[side, step, m],
            recv_sem=recv.at[side, step, m],
            device_id={"dp": me - 1 if side == 0 else me + 1},
            device_id_type=MESH,
        )

    def sends(side, step):
        if side == 0:
            return jnp.logical_and(me < count - 1, me - step >= 0)
        return jnp.logical_and(me > 0, me + step <= count - 1)

    def arrives(side, step):
        return me - 1 - step >= 0 if side == 0 else me + 1 + step <= count - 1

    for step in range(count - 1):
        for m in range(batches):
            for side in range(2):
                if step:

                    @pl.when(arrives(side, step - 1))
                    def _():
                        arrival(side, step - 1, m).wait_recv()

                @pl.when(sends(side, step))
                def _():
                    copy(side, step, m).start()

    for m in range(batches):
        for side in range(2):

            @pl.when(arrives(side, count - 2))
            def _():
                arrival(side, count - 2, m).wait_recv()

    for step in range(count - 1):
        for m in range(batches):
            for side in range(2):

                @pl.when(sends(side, step))
                def _():
                    copy(side, step, m).wait_send()


def gather_dp(block):
    count = lax.axis_size("dp")
    batches = block.shape[0]
    if count == 1:
        return block[None]
    semaphores = pltpu.SemaphoreType.DMA((2, count - 1, batches))
    return pl.pallas_call(
        functools.partial(gather_kernel, count),
        out_shape=jax.ShapeDtypeStruct((count,) + block.shape, block.dtype),
        in_specs=[pl.BlockSpec(memory_space=pltpu.VMEM)],
        out_specs=pl.BlockSpec(memory_space=pltpu.VMEM),
        scratch_shapes=[semaphores, semaphores],
        compiler_params=pltpu.CompilerParams(
            collective_id=1, has_side_effects=True, vmem_limit_bytes=VMEM_BYTES
        ),
    )(block)


def scatter_kernel(count, x_ref, o_ref, landed, send, recv):
    me = lax.axis_index("dp")
    batches = x_ref.shape[1]
    meet_line("dp", me, count)

    def copy(side, step, m, source):
        return pltpu.make_async_remote_copy(
            src_ref=source,
            dst_ref=landed.at[side, step, m],
            send_sem=send.at[side, step, m],
            recv_sem=recv.at[side, step, m],
            device_id={"dp": me + 1 if side == 0 else me - 1},
            device_id_type=MESH,
        )

    for step in range(count - 1):
        for m in range(batches):
            for side in range(2):
                owner = count - 1 - step if side == 0 else step

                @pl.when(me == 0 if side == 0 else me == count - 1)
                def _():
                    copy(side, step, m, x_ref.at[owner, m]).start()

    items = (count - 1) * batches
    for slot in range(1, items + count - 2):
        for side in range(2):
            item = slot - (me if side == 0 else count - 1 - me)
            step = lax.div(item, batches)
            m = item - step * batches
            owner = count - 1 - step if side == 0 else step
            moves = me < owner if side == 0 else me > owner
            inner = me > 0 if side == 0 else me < count - 1
            valid = jnp.logical_and(item >= 0, item < items)

            @pl.when(jnp.logical_and(jnp.logical_and(inner, valid), moves))
            def _():
                copy(side, step, m, landed.at[side, step, m]).wait_recv()
                landed[side, step, m] = (
                    landed[side, step, m].astype(jnp.float32)
                    + x_ref[owner, m].astype(jnp.float32)
                ).astype(jnp.bfloat16)
                copy(side, step, m, landed.at[side, step, m]).start()

    for m in range(batches):
        o_ref[m] = x_ref[me, m].astype(jnp.float32)
        for side in range(2):
            step = count - 1 - me if side == 0 else me

            @pl.when(me > 0 if side == 0 else me < count - 1)
            def _():
                copy(side, step, m, landed.at[side, step, m]).wait_recv()
                o_ref[m] += landed[side, step, m].astype(jnp.float32)

    for step in range(count - 1):
        for m in range(batches):
            for side in range(2):
                owner = count - 1 - step if side == 0 else step

                @pl.when(me < owner if side == 0 else me > owner)
                def _():
                    copy(side, step, m, x_ref.at[owner, m]).wait_send()


def scatter_dp(terms):
    count, batches, rows, width = terms.shape
    if count == 1:
        return terms[0].astype(jnp.float32)
    semaphores = pltpu.SemaphoreType.DMA((2, count - 1, batches))
    return pl.pallas_call(
        functools.partial(scatter_kernel, count),
        out_shape=jax.ShapeDtypeStruct((batches, rows, width), jnp.float32),
        in_specs=[pl.BlockSpec(memory_space=pltpu.VMEM)],
        out_specs=pl.BlockSpec(memory_space=pltpu.VMEM),
        scratch_shapes=[
            pltpu.VMEM((2, count - 1, batches, rows, width), jnp.bfloat16),
            semaphores,
            semaphores,
        ],
        compiler_params=pltpu.CompilerParams(
            collective_id=2, has_side_effects=True, vmem_limit_bytes=VMEM_BYTES
        ),
    )(terms.astype(jnp.bfloat16))


def layer_forward(inputs, allowed, params):
    (
        gains,
        biases,
        qkv_weight,
        qv_bias,
        out_weight,
        out_bias,
        fc_weight,
        fc_bias,
        proj_weight,
        proj_bias,
    ) = params
    batches, _, shard_rows, key_count = allowed.shape
    local_width = qkv_weight.shape[2]
    head_count = local_width // HEAD
    normed = layer_norm(inputs, gains[0], biases[0]).astype(jnp.bfloat16)
    projected = jnp.dot(
        normed,
        qkv_weight.reshape(qkv_weight.shape[0], 3 * local_width),
        preferred_element_type=jnp.float32,
    )
    query = (projected[:, :local_width] + qv_bias[0]).astype(jnp.bfloat16)
    keys = projected[:, local_width : 2 * local_width].astype(jnp.bfloat16)
    values = (projected[:, 2 * local_width :] + qv_bias[1]).astype(jnp.bfloat16)
    pair = jnp.concatenate([keys, values], axis=1).reshape(batches, shard_rows, 2 * local_width)
    gathered = gather_dp(pair)
    gathered = gathered.transpose(1, 0, 2, 3).reshape(batches, key_count, 2, head_count, HEAD)
    key_heads = gathered[:, :, 0]
    value_heads = gathered[:, :, 1]
    queries = query.reshape(batches, shard_rows, head_count, HEAD)
    scores = jnp.einsum(
        "mqhe,mkhe->mhqk", queries, key_heads, preferred_element_type=jnp.float32
    ) * (1.0 / math.sqrt(HEAD))
    scores = jnp.where(allowed, scores, MASKED)
    peak = jnp.max(scores, axis=-1, keepdims=True)
    powers = jnp.where(allowed, jnp.exp(scores - peak), 0.0)
    softmax = powers / jnp.sum(powers, axis=-1, keepdims=True)
    attended = jnp.einsum(
        "mhqk,mkhe->mqhe",
        softmax.astype(jnp.bfloat16),
        value_heads,
        preferred_element_type=jnp.float32,
    )
    attended = attended.reshape(batches * shard_rows, local_width).astype(jnp.bfloat16)
    middle = (
        inputs
        + sum_tensor(jnp.dot(attended, out_weight, preferred_element_type=jnp.float32))
        + out_bias
    )
    normed_mid = layer_norm(middle, gains[1], biases[1]).astype(jnp.bfloat16)
    hidden_pre = jnp.dot(normed_mid, fc_weight, preferred_element_type=jnp.float32) + fc_bias
    active = gelu_tanh(hidden_pre).astype(jnp.bfloat16)
    output = (
        middle
        + sum_tensor(jnp.dot(active, proj_weight, preferred_element_type=jnp.float32))
        + proj_bias
    )
    saved_state = (
        inputs,
        normed,
        queries,
        key_heads,
        value_heads,
        softmax,
        attended,
        middle,
        normed_mid,
        hidden_pre,
        active,
    )
    return (output, saved_state)


def layer_backward(grad_output, saved_state, params, with_grads):
    (
        gains,
        biases,
        qkv_weight,
        qv_bias,
        out_weight,
        out_bias,
        fc_weight,
        fc_bias,
        proj_weight,
        proj_bias,
    ) = params
    (
        inputs,
        normed,
        queries,
        key_heads,
        value_heads,
        softmax,
        attended,
        middle,
        normed_mid,
        hidden_pre,
        active,
    ) = saved_state
    batches, shard_rows, head_count, _ = queries.shape
    rows = batches * shard_rows
    local_width = head_count * HEAD
    key_count = key_heads.shape[1]
    score_scale = 1.0 / math.sqrt(HEAD)

    grad_low = grad_output.astype(jnp.bfloat16)
    grad_active = contract_cols(grad_low, proj_weight)
    grad_pre = jax.vjp(gelu_tanh, hidden_pre)[1](grad_active)[0].astype(jnp.bfloat16)
    partial_mid = contract_cols(grad_pre, fc_weight)
    if with_grads:
        grad_proj_weight = contract_rows(active, grad_low).astype(jnp.bfloat16)
        grad_fc_weight = contract_rows(normed_mid, grad_pre).astype(jnp.bfloat16)
        partial_mid, grad_proj_weight, grad_fc_weight = lax.optimization_barrier(
            (partial_mid, grad_proj_weight, grad_fc_weight)
        )
        early = lax.psum((grad_proj_weight, grad_fc_weight), "dp")
    grad_normed_mid = sum_tensor(partial_mid)
    grad_middle_norm, grad_gain_mid, grad_bias_mid = jax.vjp(
        layer_norm, middle, gains[1], biases[1]
    )[1](grad_normed_mid)
    grad_middle = grad_output + grad_middle_norm
    middle_low = grad_middle.astype(jnp.bfloat16)
    grad_attended = contract_cols(middle_low, out_weight).astype(jnp.bfloat16)
    if with_grads:
        grad_out_weight = contract_rows(attended, middle_low).astype(jnp.bfloat16)
    grad_heads = grad_attended.reshape(batches, shard_rows, head_count, HEAD)
    grad_softmax = jnp.einsum(
        "mqhe,mkhe->mhqk", grad_heads, value_heads, preferred_element_type=jnp.float32
    )
    delta = jnp.sum(softmax * grad_softmax, axis=-1, keepdims=True)
    grad_scores = (softmax * (grad_softmax - delta)).astype(jnp.bfloat16)
    grad_query = (
        jnp.einsum("mhqk,mkhe->mqhe", grad_scores, key_heads, preferred_element_type=jnp.float32)
        * score_scale
    )
    grad_keys = (
        jnp.einsum("mhqk,mqhe->mkhe", grad_scores, queries, preferred_element_type=jnp.float32)
        * score_scale
    )
    grad_values = jnp.einsum(
        "mhqk,mqhe->mkhe",
        softmax.astype(jnp.bfloat16),
        grad_heads,
        preferred_element_type=jnp.float32,
    )
    terms = jnp.concatenate(
        [
            grad_keys.reshape(batches, key_count, local_width),
            grad_values.reshape(batches, key_count, local_width),
        ],
        axis=2,
    ).astype(jnp.bfloat16)
    terms = terms.reshape(batches, key_count // shard_rows, shard_rows, 2 * local_width)
    key_grads = scatter_dp(terms.transpose(1, 0, 2, 3)).reshape(rows, 2 * local_width)
    grad_query = grad_query.reshape(rows, local_width).astype(jnp.bfloat16)
    grad_keys = key_grads[:, :local_width].astype(jnp.bfloat16)
    grad_values = key_grads[:, local_width:].astype(jnp.bfloat16)
    grad_projected = jnp.concatenate([grad_query, grad_keys, grad_values], axis=1)
    qkv_flat = qkv_weight.reshape(qkv_weight.shape[0], -1)
    if with_grads:
        grad_qkv_weight = contract_rows(normed, grad_projected).astype(jnp.bfloat16)
    grad_normed = sum_tensor(contract_cols(grad_projected, qkv_flat))
    grad_input_norm, grad_gain_in, grad_bias_in = jax.vjp(layer_norm, inputs, gains[0], biases[0])[
        1
    ](grad_normed)
    grad_input = grad_middle + grad_input_norm
    if not with_grads:
        return (grad_input, None)
    small = jnp.concatenate(
        [
            grad_gain_in,
            grad_gain_mid,
            grad_bias_in,
            grad_bias_mid,
            jnp.sum(grad_query.astype(jnp.float32), axis=0),
            jnp.sum(grad_values.astype(jnp.float32), axis=0),
            jnp.sum(grad_middle, axis=0),
            jnp.sum(grad_pre.astype(jnp.float32), axis=0),
            jnp.sum(grad_output, axis=0),
        ]
    ).astype(jnp.bfloat16)
    columns = 3 * local_width
    small_rows = -(-small.shape[0] // columns)
    small = jnp.pad(small, (0, small_rows * columns - small.shape[0]))
    late = jnp.concatenate([grad_qkv_weight, small.reshape(small_rows, columns)], axis=0)
    late, grad_out_weight, early = lax.optimization_barrier((late, grad_out_weight, early))
    late, grad_out_weight = lax.psum((late, grad_out_weight), "dp")
    late = late.astype(jnp.float32)
    grad_out_weight = grad_out_weight.astype(jnp.float32)
    grad_proj_weight, grad_fc_weight = (member.astype(jnp.float32) for member in early)
    grad_qkv_weight = late[: qkv_weight.shape[0]]
    small = late[qkv_weight.shape[0] :].reshape(-1)
    width = gains.shape[1]
    sizes = (2 * width, 2 * width, 2 * local_width, width, fc_bias.shape[0], width)
    parts = []
    begin = 0
    for size in sizes:
        parts.append(small[begin : begin + size])
        begin += size
    grads = (
        parts[0].reshape(gains.shape),
        parts[1].reshape(biases.shape),
        grad_qkv_weight.reshape(qkv_weight.shape),
        parts[2].reshape(qv_bias.shape),
        grad_out_weight,
        parts[3],
        grad_fc_weight,
        parts[4],
        grad_proj_weight,
        parts[5],
    )
    return (grad_input, grads)


def per_device(
    tokens,
    block_order,
    ln_gain,
    ln_bias,
    qkv_weight,
    qv_bias,
    out_weight,
    out_bias,
    fc_weight,
    fc_bias,
    proj_weight,
    proj_bias,
    cotangent,
):
    micro_count, shard_rows, model_width = tokens.shape
    is_first = lax.axis_index("section") == 0
    dp_index = lax.axis_index("dp")
    params = (
        ln_gain[0],
        ln_bias[0],
        qkv_weight[0],
        qv_bias[0],
        out_weight[0],
        out_bias[0],
        fc_weight[0],
        fc_bias[0],
        proj_weight[0],
        proj_bias[0],
    )
    row_offsets = jnp.arange(shard_rows, dtype=jnp.int32)
    positions = block_order[:, :, None] * shard_rows + row_offsets
    key_pos = positions.reshape(micro_count, -1)
    query_pos = block_order[:, dp_index][:, None] * shard_rows + row_offsets
    allowed = (query_pos[:, :, None] >= key_pos[:, None, :])[:, None]
    rows = micro_count * shard_rows
    inputs = tokens.reshape(rows, model_width).astype(jnp.float32)
    output, _ = layer_forward(inputs, allowed, params)
    received = swap_sections(output.astype(jnp.bfloat16)).astype(jnp.float32)
    inputs = jnp.where(is_first, inputs, received)
    output, saved_state = layer_forward(inputs, allowed, params)
    seed_grad = cotangent.reshape(rows, model_width).astype(jnp.float32)
    grad_input, _ = layer_backward(seed_grad, saved_state, params, False)
    received = swap_sections(grad_input.astype(jnp.bfloat16)).astype(jnp.float32)
    grad_output = jnp.where(is_first, received, seed_grad)
    grad_input, grads = layer_backward(grad_output, saved_state, params, True)
    section_out = output.astype(jnp.bfloat16).reshape(tokens.shape)[None]
    section_grad = grad_input.reshape(tokens.shape)[None]
    return (section_out, section_grad) + tuple((member[None] for member in grads))


def solution(mesh):
    return jax.shard_map(
        per_device,
        mesh=mesh,
        in_specs=(
            P(None, "dp", None),
            P(),
            P("section", None, None),
            P("section", None, None),
            P("section", None, None, "tensor"),
            P("section", None, "tensor"),
            P("section", "tensor", None),
            P("section", None),
            P("section", None, "tensor"),
            P("section", "tensor"),
            P("section", "tensor", None),
            P("section", None),
            P(None, "dp", None),
        ),
        out_specs=(
            P("section", None, "dp", None),
            P("section", None, "dp", None),
            P("section", None, None),
            P("section", None, None),
            P("section", None, None, "tensor"),
            P("section", None, "tensor"),
            P("section", "tensor", None),
            P("section", None),
            P("section", None, "tensor"),
            P("section", "tensor"),
            P("section", "tensor", None),
            P("section", None),
        ),
        check_vma=False,
    )
```
